256 devices in a mesh: chan: 4 (over z_lo), seq: 64 (over x, y, z_hi, core).
Axes of the slice: x: 4, y: 4, z: 8 (z_hi: 2, z_lo: 4; z = z_hi * 4 + z_lo), core: 2. Of those that a mesh axis runs over, the one named last changes fastest.
Arguments:
- ids: int32 [16384], P('seq'), may hold values from 0 to 511
- embed_proj: bfloat16 [512, 3, 4096], P(None, None, 'chan'), may hold values from -6 to 6
- short_filter: float32 [7, 3, 4096], P(None, None, 'chan'), may hold values from -2 to 2
- mr_filter: bfloat16 [256, 128], replicated, may hold values from -0.5 to 0.5
- li_proj: bfloat16 [4096, 3, 4096], P('seq', None, 'chan'), may hold values from -0.09375 to 0.09375
- residue: float32 [256, 16], replicated, may hold values from -1.5 to 1.5
- rate: float32 [256, 16], replicated, may hold values from 0.5 to 512
- out_proj: bfloat16 [4096, 512], P('chan'), may hold values from -0.09375 to 0.09375
Outputs:
- logits: bfloat16 [16384, 512], P('seq', 'chan')
The draws below stay inside these ranges and needn't reach their ends.
All inputs are finite; a program needn't handle non-finite values.
Results may differ from the reference program's by a relative error of at most 0.015.
Values may be sent and summed in bfloat16 or wider, within the bound.
No kernel may reach another device: no remote copies, remote signals or barrier semaphores. Data moves between devices by JAX's collectives and lax.ppermute only.
A program may use at most 192 MiB of HBM per device.

```python
import math
import jax
import jax.numpy as jnp
from jax import lax

V = 512
CH = 4096
GSIZE = 16
MRTAPS = 128
SHORT = 7
MODES = 16
GROUPS = 256
TOKENS = 16384


def set_ends(drawn, rng, low, largest):
    longest = drawn.shape.index(max(drawn.shape))
    spots = []
    for shift in (0, 1):
        where = [jax.random.randint(jax.random.fold_in(rng, axis), (), 0, length) for axis, length in enumerate(drawn.shape)]
        where[longest] = (where[longest] + shift) % drawn.shape[longest]
        spots.append(tuple(where))
    return drawn.at[spots[0]].set(low).at[spots[1]].set(largest)


def level_of(key, shape, split, least, top_value):
    gain = 1.0
    for dim, parts in split:
        steps = jax.random.uniform(jax.random.fold_in(jax.random.fold_in(key, 6), dim), (parts,), jnp.float32, least / len(split), top_value / len(split))
        gain = gain * jnp.repeat(jnp.exp(steps), shape[dim] // parts).reshape((-1,) + (1,) * (len(shape) - 1 - dim))
    return gain


def bell_draw(own_key, extent, scale, most, split=(), kind=jnp.bfloat16):
    values = scale * jax.random.normal(own_key, extent, jnp.float32)
    if split:
        values = values * level_of(own_key, extent, split, -0.22, 0.18)
    return jnp.clip(values, -most, most).astype(kind)


def setup_inputs(seed: int = 0) -> dict:
    key_of = jax.random.split(jax.random.key(seed), 9)
    return {
        "ids": set_ends(jax.random.randint(key_of[0], (TOKENS,), 0, V), jax.random.fold_in(key_of[0], 1), 0, V - 1).astype(jnp.int32),
        "embed_proj": bell_draw(key_of[1], (V, 3, CH), 1.0, 6.0, ((2, 4),)),
        "short_filter": bell_draw(key_of[2], (SHORT, 3, CH), SHORT ** -0.5, 2.0, ((2, 4),), jnp.float32),
        "mr_filter": bell_draw(key_of[3], (GROUPS, MRTAPS), MRTAPS ** -0.5, 0.5),
        "li_proj": bell_draw(key_of[4], (CH, 3, CH), CH ** -0.5, 0.09375, ((0, 64), (2, 4))),
        "residue": bell_draw(key_of[5], (GROUPS, MODES), 0.25, 1.5, (), jnp.float32),
        "rate": jnp.clip(jnp.exp(jax.random.uniform(key_of[6], (GROUPS, MODES), jnp.float32, math.log(0.5), math.log(512.0))), 0.5, 512.0),
        "out_proj": bell_draw(key_of[7], (CH, V), CH ** -0.5, 0.09375, ((0, 4),)),
    }


def band_matrix(filt, block):
    groups, taps = filt.shape
    period = 2 * block + taps
    cols = block + taps - 1
    padded = jnp.concatenate([filt, jnp.zeros((groups, period - taps), filt.dtype)], axis=1)
    tiled = jnp.tile(padded, (1, cols))[:, :cols * (period - 1)]
    skewed = tiled.reshape(groups, cols, period - 1)
    return jnp.swapaxes(skewed[:, :, taps - 1:taps - 1 + block], 1, 2)

def medium_apply(padded, filt, block):
    taps = filt.shape[1]
    rows = padded.shape[0] - (taps - 1)
    groups = filt.shape[0]
    width = padded.shape[1]
    gsize = width // groups
    nblock = rows // block
    own = padded[taps - 1:].reshape(nblock, block, groups, gsize)
    prev = padded[:rows].reshape(nblock, block, groups, gsize)[:, :taps - 1]
    full = band_matrix(filt, block)
    tail = full[:, :, :taps - 1]
    main = full[:, :, taps - 1:]
    out = jnp.einsum('gij,njgc->nigc', main, own, preferred_element_type=jnp.float32)
    out = out + jnp.einsum('gij,njgc->nigc', tail, prev, preferred_element_type=jnp.float32)
    return out.reshape(rows, width)

def modal_conv(signal, coef, loglam, block):
    fcount, mcount, rows = signal.shape
    nblock = rows // block
    blocked = signal.reshape(fcount, mcount, nblock, block)
    index = jnp.arange(block)
    lag = index[:, None] - index[None, :]
    lagf = jnp.maximum(lag, 0).astype(jnp.float32)
    kernel = jnp.zeros((fcount, block, block), jnp.float32)
    for mode in range(coef.shape[1]):
        kernel = kernel + coef[:, mode, None, None] * jnp.exp(lagf[None] * loglam[:, mode, None, None])
    kernel = jnp.where(lag[None] >= 0, kernel, jnp.zeros((), jnp.float32))
    inner = jnp.einsum('fij,fmnj->fmni', kernel, blocked, precision=lax.Precision.HIGH)
    fade = jnp.exp((block - 1 - index).astype(jnp.float32)[None, None, :] * loglam[:, :, None])
    local = jnp.einsum('fsj,fmnj->fsmn', fade, blocked, precision=lax.Precision.HIGH)
    factor = jnp.broadcast_to(jnp.exp(block * loglam)[:, :, None, None], local.shape)

    def combine(early, later):
        return (early[0] * later[0], later[0] * early[1] + later[1])
    inclusive = lax.associative_scan(combine, (factor, local), axis=3)[1]
    starts = jnp.concatenate([jnp.zeros_like(inclusive[..., :1]), inclusive[..., :-1]], axis=3)
    leading = coef[:, :, None] * jnp.exp((index + 1).astype(jnp.float32)[None, None, :] * loglam[:, :, None])
    cross = jnp.einsum('fsi,fsmn->fmni', leading, starts, precision=lax.Precision.HIGHEST)
    return ((inner + cross).reshape(fcount, mcount, rows), inclusive[..., -1])

def reference(ids, embed_proj, short_filter, mr_filter, li_proj, residue, rate, out_proj):
    length = ids.shape[0]
    onehot = (ids[:, None] == jnp.arange(V)[None, :]).astype(jnp.bfloat16)
    feats = jnp.dot(onehot, embed_proj.reshape(V, 3 * CH), preferred_element_type=jnp.float32).reshape(length, 3, CH)
    reach = MRTAPS + SHORT - 2
    feats = jnp.concatenate([jnp.zeros((reach, 3, CH), jnp.float32), feats], axis=0)
    count = length + MRTAPS - 1
    short = jnp.zeros((count, 3, CH), jnp.float32)
    for tap in range(SHORT):
        short = short + short_filter[tap] * feats[SHORT - 1 - tap:SHORT - 1 - tap + count]
    gated = (short[:, 0] * short[:, 1]).astype(jnp.bfloat16)
    keep = jnp.arange(count) >= MRTAPS - 1
    gated = jnp.where(keep[:, None], gated, jnp.zeros((), jnp.bfloat16))
    medium = medium_apply(gated, mr_filter, min(512, length))
    mr_out = (short[MRTAPS - 1:, 2] * medium).astype(jnp.bfloat16)
    li = jnp.dot(mr_out, li_proj.reshape(CH, 3 * CH), preferred_element_type=jnp.float32).reshape(length, 3, CH)
    mixed = (li[:, 1] * li[:, 2]).astype(jnp.bfloat16)
    loglam = -rate / TOKENS
    coef = residue * jnp.sqrt(-jnp.expm1(2.0 * loglam))
    signal = mixed.astype(jnp.float32).T.reshape(GROUPS, GSIZE, length)
    result, _ = modal_conv(signal, coef, loglam, min(512, length))
    longer = result.reshape(CH, length).T
    li_out = (li[:, 0] * longer).astype(jnp.bfloat16)
    return jnp.dot(li_out, out_proj, preferred_element_type=jnp.float32).astype(jnp.bfloat16)
```

```python
import functools

import jax
import jax.numpy as jnp
from jax import lax
from jax.experimental import pallas as pl
from jax.experimental.pallas import tpu as pltpu
from jax.sharding import Mesh
from jax.sharding import PartitionSpec as P

F32 = jnp.float32
BF16 = jnp.bfloat16
GSIZE = 16
NX, NY, NH, NC, NL = 4, 4, 2, 2, 4
NZ = NH * NL
SEQ = ("x", "y", "run", "core")
HALO = 144
HIGHEST = lax.Precision.HIGHEST


def seq_of(x, y, h, c):
    return ((x * NY + y) * NH + h) * NC + c


COORDS = [
    (x, y, h, c) for x in range(NX) for y in range(NY) for h in range(NH) for c in range(NC)
]


def seq_pairs(move):
    return [(seq_of(*a), seq_of(*move(*a))) for a in COORDS]


def from_x(v, j):
    return lax.ppermute(v, SEQ, seq_pairs(lambda x, y, h, c: ((x - j) % NX, y, h, c)))


def from_y(v, j):
    return lax.ppermute(v, SEQ, seq_pairs(lambda x, y, h, c: (x, (y - j) % NY, h, c)))


def from_run(v):
    return lax.ppermute(v, SEQ, seq_pairs(lambda x, y, h, c: (x, y, 1 - h, c)))


def from_core(v):
    return lax.ppermute(v, SEQ, seq_pairs(lambda x, y, h, c: (x, y, h, 1 - c)))


def from_x_before(v, j):
    pairs = [(seq_of(x, y, h, c), seq_of(x + j, y, h, c)) for x, y, h, c in COORDS if x + j < NX]
    return lax.ppermute(v, SEQ, pairs)


def to_z(v, d):
    pairs = []
    for z in range(NZ):
        for x in range(NX):
            for y in range(NY):
                for c in range(NC):
                    t = (z + d) % NZ
                    pairs.append(
                        (
                            (z % NL) * len(COORDS) + seq_of(x, y, z // NL, c),
                            (t % NL) * len(COORDS) + seq_of(x, y, t // NL, c),
                        )
                    )
    return lax.ppermute(v, ("chan",) + SEQ, pairs)


def act_kernel(
    where, ids_ref, emb_ref, sf_ref, mr_ref, keep_ref, send_ref, hot, feats, bands, held
):
    rows = keep_ref.shape[0]
    ext = hot.shape[0]
    step = pl.program_id(0)
    core = where[3]
    yy = lax.rem(where[1] + step, NY)
    wide = pl.ds(pl.multiple_of(yy * 256, 256), 256)

    @pl.when(step == 0)
    def _():
        col = lax.broadcasted_iota(jnp.int32, hot.shape, 1)
        hot[...] = jnp.where(ids_ref[...] == col, 1.0, 0.0).astype(BF16)

    for j in range(3):
        feats[j] = jnp.dot(hot[...], emb_ref[j, :, wide], preferred_element_type=F32)

    reach = 128
    group = (lax.broadcasted_iota(jnp.int32, (128, 256), 1) // GSIZE) % 8
    for b in range(2):
        cols = slice(b * 128, (b + 1) * 128)
        lanes = pl.ds(pl.multiple_of(yy * 256 + b * 128, 128), 128)

        def short(j, start, n, cols=cols, lanes=lanes):
            total = sf_ref[j, 0:1, lanes] * feats[j, start : start + n, cols]
            for k in range(1, 7):
                tap = sf_ref[j, k : k + 1, lanes]
                total = total + tap * feats[j, start - k : start - k + n, cols]
            return total

        first = ext - rows - reach
        gated = (short(0, first, rows + reach) * short(1, first, rows + reach)).astype(BF16)
        window = jnp.concatenate([gated[:256], gated[128:384]], axis=1)
        filt = mr_ref[pl.ds(pl.multiple_of(yy * 16 + b * 8, 8), 8), :]
        for g in range(8):
            base = jnp.broadcast_to(filt[g : g + 1, :], (128, 256))
            bands[g * 128 : (g + 1) * 128, :] = pltpu.roll(
                base, 0, 1, stride=1, stride_axis=0
            ).astype(BF16)
        both = jnp.dot(bands[...], window, preferred_element_type=F32)
        medium = both[:128]
        for g in range(1, 8):
            medium = jnp.where(group == g, both[g * 128 : (g + 1) * 128], medium)
        v1 = short(2, ext - rows, rows)
        out = jnp.concatenate([v1[:128] * medium[:, :128], v1[128:] * medium[:, 128:]], axis=0)

        @pl.when(lax.rem(step, 2) == 0)
        def _(out=out, b=b):
            held[b] = out

        @pl.when(lax.rem(step, 2) == 1)
        def _(out=out, b=b):
            even = jnp.concatenate([held[b, :, :64], out[:, :64]], axis=1)
            odd = jnp.concatenate([held[b, :, 64:], out[:, 64:]], axis=1)
            to = pl.ds(pl.multiple_of(b * 256 + (step // 2) * 128, 128), 128)
            keep_ref[:, to] = jnp.where(core == 0, even, odd).astype(BF16)
            send_ref[:, to] = jnp.where(core == 0, odd, even).astype(BF16)


def activations(where, ids, emb, sf, mr_rows):
    ext = ids.shape[0]
    return pl.pallas_call(
        act_kernel,
        grid=(4,),
        out_shape=(jax.ShapeDtypeStruct((256, 512), BF16),) * 2,
        in_specs=[
            pl.BlockSpec(memory_space=pltpu.SMEM),
            pl.BlockSpec(memory_space=pltpu.VMEM),
            pl.BlockSpec(memory_space=pltpu.VMEM),
            pl.BlockSpec(memory_space=pltpu.VMEM),
            pl.BlockSpec(memory_space=pltpu.VMEM),
        ],
        out_specs=(pl.BlockSpec(memory_space=pltpu.VMEM),) * 2,
        scratch_shapes=[
            pltpu.VMEM((ext, 512), BF16),
            pltpu.VMEM((3, ext, 256), F32),
            pltpu.VMEM((1024, 256), BF16),
            pltpu.VMEM((2, 256, 128), F32),
        ],
        compiler_params=pltpu.CompilerParams(vmem_limit_bytes=12 * 2**20),
        cost_estimate=pl.CostEstimate(flops=4 * 10**9, bytes_accessed=8 * 10**6, transcendentals=0),
    )(where, ids, emb, sf, mr_rows)


def toeplitz_kernel(h_ref, out_ref):
    for g in range(8):
        base = jnp.broadcast_to(h_ref[g : g + 1, :], (256, 512))
        out_ref[g] = pltpu.roll(base, 0, 1, stride=1, stride_axis=0)[:, :256].astype(BF16)


def toeplitz(base_rows):
    groups = base_rows.shape[0]
    return pl.pallas_call(
        toeplitz_kernel,
        grid=(groups // 8,),
        out_shape=jax.ShapeDtypeStruct((groups, 256, 256), BF16),
        in_specs=[pl.BlockSpec((8, 512), lambda i: (i, 0))],
        out_specs=pl.BlockSpec((8, 256, 256), lambda i: (i, 0, 0)),
        compiler_params=pltpu.CompilerParams(vmem_limit_bytes=12 * 2**20),
        cost_estimate=pl.CostEstimate(flops=10**7, bytes_accessed=4 * 10**6, transcendentals=0),
    )(base_rows)


def block_place(where, d):
    zz = lax.rem(where[4] + d + NZ, NZ)
    rows = pl.multiple_of((zz // NL) * 256, 256)
    lanes = pl.multiple_of(lax.rem(zz, NL) * 512, 512)
    return pl.ds(rows, 256), pl.ds(lanes, 512)


def gather_kernel(steps, plan, halves, where, *refs):
    n_in = len(steps) + len(plan)
    sources = refs[:n_in]
    outs = 4 if halves else 2
    a_ref, w_ref = refs[-1 - outs], refs[-outs]
    sem = refs[-1]
    x, h = where[0], where[2]
    copies = []
    for src, (d, first, count) in zip(sources, steps):
        rows, lanes = block_place(where, d)
        for p in range(count):
            copies.append((src.at[pl.ds(p * 256, 256), :], a_ref.at[first + p, rows, lanes]))
    for src, (own_run, at) in zip(sources[len(steps) :], plan):
        run = h if own_run else 1 - h
        for other in range(4):
            j, k = (other, at) if own_run else (at, other)
            row = lax.rem(x + j, NX) * 512 + run * 256 + k * 64
            rows = pl.ds(pl.multiple_of(row, 64), 64)
            copies.append((src.at[other], w_ref.at[:, rows, :]))
    if halves:
        copies.append((sources[0].at[pl.ds(0, 256), :], refs[-3]))
        copies.append((sources[1].at[pl.ds(256, 256), :], refs[-2]))
    copies = [pltpu.make_async_copy(a, b, sem.at[n]) for n, (a, b) in enumerate(copies)]
    for copy in copies:
        copy.start()
    for copy in copies:
        copy.wait()


def gather(where, full, blocks, pieces, halves=False):
    steps = [b[:3] for b in blocks]
    plan = [(own_run, at) for own_run, at, _ in pieces]
    operands = [b[3] for b in blocks] + [v for _, _, v in pieces]
    vmem = pl.BlockSpec(memory_space=pltpu.VMEM)
    alias = {}
    if full is not None:
        alias = {1 + len(operands): 0, 2 + len(operands): 1}
        operands += list(full)
    n_copies = sum(c for _, _, c in steps) + 4 * len(plan) + 2 * halves
    shapes = (
        jax.ShapeDtypeStruct((2, 512, 2048), BF16),
        jax.ShapeDtypeStruct((3, 2048, 512), BF16),
    )
    shapes += (jax.ShapeDtypeStruct((256, 512), BF16),) * (2 * halves)
    return pl.pallas_call(
        functools.partial(gather_kernel, steps, plan, halves),
        out_shape=shapes,
        in_specs=[pl.BlockSpec(memory_space=pltpu.SMEM)] + [vmem] * len(operands),
        out_specs=(vmem,) * len(shapes),
        scratch_shapes=[pltpu.SemaphoreType.DMA((n_copies,))],
        input_output_aliases=alias,
        compiler_params=pltpu.CompilerParams(vmem_limit_bytes=4 * 2**20),
        cost_estimate=pl.CostEstimate(flops=10**6, bytes_accessed=6 * 10**6, transcendentals=0),
    )(where, *operands)


def li_kernel(which, a_ref, w_ref, out_ref):
    for t in range(3):

        def step(m, _, t=t):
            rows = pl.ds(pl.multiple_of(m * 256, 256), 256)
            out_ref[t, rows, :] = jnp.dot(
                a_ref[which, rows, :], w_ref[t], preferred_element_type=F32
            ).astype(out_ref.dtype)
            return 0

        lax.fori_loop(0, 2, step, 0)


def li_terms(which, a_full, w_full):
    vmem = pl.BlockSpec(memory_space=pltpu.VMEM)
    return pl.pallas_call(
        functools.partial(li_kernel, which),
        out_shape=jax.ShapeDtypeStruct((3, 512, 512), BF16 if which else F32),
        in_specs=[vmem] * 2,
        out_specs=vmem,
        compiler_params=pltpu.CompilerParams(vmem_limit_bytes=8 * 2**20),
        cost_estimate=pl.CostEstimate(
            flops=33 * 10**8, bytes_accessed=10 * 10**6, transcendentals=0
        ),
    )(a_full, w_full)


def states_kernel(own_ref, got_ref, fade_ref, q_ref, mixed_ref, state_ref):
    q_ref[...] = own_ref[0] + got_ref[0].astype(F32)
    group = lax.broadcasted_iota(jnp.int32, (16, 128), 1) // GSIZE
    for b in range(4):
        cols = slice(b * 128, (b + 1) * 128)
        fade = fade_ref[cols, :]
        high = fade.astype(BF16)
        low = (fade - high.astype(F32)).astype(BF16)
        for m in range(2):
            rows = slice(m * 256, (m + 1) * 256)
            k2 = own_ref[1, rows, cols] + got_ref[1, rows, cols].astype(F32)
            v2 = own_ref[2, rows, cols] + got_ref[2, rows, cols].astype(F32)
            block = (k2 * v2).astype(BF16)
            mixed_ref[rows, cols] = block
            full = jnp.dot(high, block, preferred_element_type=F32) + jnp.dot(
                low, block, preferred_element_type=F32
            )
            state = full[:16]
            for g in range(1, 8):
                state = jnp.where(group == g, full[g * 16 : (g + 1) * 16], state)
            state_ref[m, :, cols] = state


def block_states(own, got, fade):
    vmem = pl.BlockSpec(memory_space=pltpu.VMEM)
    return pl.pallas_call(
        states_kernel,
        out_shape=(
            jax.ShapeDtypeStruct((512, 512), F32),
            jax.ShapeDtypeStruct((512, 512), BF16),
            jax.ShapeDtypeStruct((2, 16, 512), F32),
        ),
        in_specs=[vmem] * 3,
        out_specs=(vmem,) * 3,
        compiler_params=pltpu.CompilerParams(vmem_limit_bytes=12 * 2**20),
        cost_estimate=pl.CostEstimate(flops=5 * 10**8, bytes_accessed=5 * 10**6, transcendentals=0),
    )(own, got, fade)


def inner_kernel(x_ref, t_ref, out_ref):
    both = jnp.concatenate([x_ref[:256, :], x_ref[256:, :]], axis=1)
    group = (lax.broadcasted_iota(jnp.int32, (256, 256), 1) // GSIZE) % 8
    total = jnp.dot(t_ref[0], both, preferred_element_type=F32)
    for g in range(1, 8):
        total = jnp.where(
            group == g, jnp.dot(t_ref[g], both, preferred_element_type=F32), total
        )
    out_ref[:256, :] = total[:, :128]
    out_ref[256:, :] = total[:, 128:]


def inner(mixed, blocks):
    return pl.pallas_call(
        inner_kernel,
        grid=(4,),
        out_shape=jax.ShapeDtypeStruct((512, 512), F32),
        in_specs=[
            pl.BlockSpec((512, 128), lambda i: (0, i)),
            pl.BlockSpec((8, 256, 256), lambda i: (i, 0, 0)),
        ],
        out_specs=pl.BlockSpec((512, 128), lambda i: (0, i)),
        compiler_params=pltpu.CompilerParams(vmem_limit_bytes=12 * 2**20),
        cost_estimate=pl.CostEstimate(
            flops=43 * 10**8, bytes_accessed=6 * 10**6, transcendentals=0
        ),
    )(mixed, blocks)


def logits_kernel(start_ref, inner_ref, q_ref, log_ref, coef_ref, proj_ref, out_ref, li_out):
    step = (lax.broadcasted_iota(jnp.int32, (256, 128), 0) + 1).astype(F32)
    row_group = lax.broadcasted_iota(jnp.int32, (128, 128), 0) // 16
    col_group = lax.broadcasted_iota(jnp.int32, (128, 128), 1) // GSIZE
    for b in range(4):
        cols = slice(b * 128, (b + 1) * 128)
        lead = coef_ref[:, cols] * jnp.exp(step * log_ref[:, cols])
        for m in range(2):
            tiled = jnp.concatenate([start_ref[m, :, cols]] * 8, axis=0)
            diag = jnp.where(row_group == col_group, tiled, 0.0)
            cross = jnp.dot(lead, diag, precision=HIGHEST, preferred_element_type=F32)
            rows = slice(m * 256, (m + 1) * 256)
            li_out[rows, cols] = (
                q_ref[rows, cols] * (inner_ref[rows, cols] + cross)
            ).astype(BF16)
    for m in range(2):
        part = jnp.dot(
            li_out[m * 256 : (m + 1) * 256, :], proj_ref[...], preferred_element_type=F32
        )
        for v in range(NL):
            out_ref[m * NL + v] = part[:, v * 128 : (v + 1) * 128].astype(BF16)


def logit_terms(start, inside, q2, log_row, coef_row, proj):
    vmem = pl.BlockSpec(memory_space=pltpu.VMEM)
    return pl.pallas_call(
        logits_kernel,
        out_shape=jax.ShapeDtypeStruct((NZ, 256, 128), BF16),
        in_specs=[vmem] * 6,
        out_specs=vmem,
        scratch_shapes=[pltpu.VMEM((512, 512), BF16)],
        compiler_params=pltpu.CompilerParams(vmem_limit_bytes=12 * 2**20),
        cost_estimate=pl.CostEstimate(
            flops=10**9, bytes_accessed=4 * 10**6, transcendentals=10**5
        ),
    )(start, inside, q2, log_row, coef_row, proj)


def shards(ids, embed_proj, short_filter, mr_filter, li_proj, residue, rate, out_proj):
    seq = lax.axis_index(SEQ)
    chan = lax.axis_index("chan")
    x, y, h, c = seq // 16, (seq // 4) % 4, (seq // 2) % 2, seq % 2
    z = h * NL + chan
    where = jnp.stack([x, y, h, c, z]).astype(jnp.int32)
    total_len = ids.shape[0] * lax.axis_size(SEQ)
    tie = lax.optimization_barrier

    halo = lax.ppermute(
        ids[ids.shape[0] - HALO :] + 1, SEQ, [(i, i + 1) for i in range(len(COORDS) - 1)]
    )
    weights = jnp.transpose(li_proj, (1, 0, 2))
    mine = lax.dynamic_slice_in_dim(weights, h * 512, 512, 2)
    theirs = lax.dynamic_slice_in_dim(weights, (1 - h) * 512, 512, 2)
    rows_b = from_run(theirs)
    ext_ids = jnp.concatenate([halo - 1, ids])[:, None]
    emb = jnp.transpose(embed_proj, (1, 0, 2))
    taps = jnp.transpose(short_filter, (1, 0, 2))
    filt = lax.dynamic_slice_in_dim(mr_filter, chan * 64, 64, 0).astype(F32)
    mr_rows = jnp.pad(filt[:, ::-1], ((0, 0), (1, 127)))
    keep, send = activations(where, ext_ids, emb, taps, mr_rows)
    keep, send, mine, rows_b = tie((keep, send, mine, rows_b))
    rate, residue, out_proj, keep = tie((rate, residue, out_proj, keep))
    first = chan * 64 + h * 32
    log_all = -lax.dynamic_slice_in_dim(rate, first, 32, 0) / total_len
    coef = lax.dynamic_slice_in_dim(residue, first, 32, 0) * jnp.sqrt(-jnp.expm1(2.0 * log_all))
    lag = (512 - jnp.arange(512)) % 512
    power = jnp.exp(lag.astype(F32)[None, None, :] * log_all[:, :, None])
    base_rows = jnp.where(lag[None, :] < 256, jnp.sum(coef[:, :, None] * power, axis=1), 0.0)
    blocks = toeplitz(base_rows)
    log_row = log_all.reshape(1, 512)
    coef_row = coef.reshape(1, 512)
    fade = jnp.exp(log_all.reshape(512, 1) * (255 - jnp.arange(256)).astype(F32)[None, :])
    log_ch = tie(jnp.repeat(log_all.T, GSIZE, axis=1))

    def decay(steps, keep=True):
        return jnp.where(keep, jnp.exp(steps * log_ch), 0.0)

    rows_of = 4.0 * ids.shape[0]
    one, row_step = decay(256.0), decay(4096.0)
    to_row = decay(rows_of * y.astype(F32))
    before = [decay(rows_of * (d - 1), d <= y) for d in (1, 2, 3)]
    within = [decay(rows_of * (3 - (y - d) % 4).astype(F32)) for d in range(4)]
    proj = lax.dynamic_slice_in_dim(out_proj, h * 512, 512, 0)
    own = jnp.concatenate([keep, from_core(send)], axis=0)

    a_x = jnp.stack([mine] + [from_x(mine, j) for j in (1, 2, 3)])
    b_y = jnp.stack([rows_b] + [from_y(rows_b, k) for k in (1, 2, 3)])
    up1, down1 = to_z(own, 1), to_z(own, -1)
    params = (fade, one, row_step, to_row, before, within, log_row, coef_row, proj, blocks)
    up1, down1, a_x, b_y, params = tie((up1, down1, a_x, b_y, params))
    fade, one, row_step, to_row, before, within, log_row, coef_row, proj, blocks = params
    full = gather(where, None, [(0, 0, 2, own)], [(True, 0, a_x), (False, 0, b_y)])
    up2, down2 = to_z(up1, 1), to_z(down1, -1)
    x2, y1, y3 = from_x(b_y, 2), from_y(a_x, 1), from_y(a_x, 3)
    full = gather(where, full, [(-1, 0, 2, up1), (1, 0, 2, down1)], [])
    up2, down2, x2, y1, y3, a_x, b_y, full = tie((up2, down2, x2, y1, y3, a_x, b_y, full))
    up3, down3 = to_z(up2, 1), to_z(down2, -1)
    x1, x3, y2 = from_x(b_y, 1), from_x(b_y, 3), from_y(a_x, 2)
    full = gather(
        where, full, [(-2, 0, 2, up2), (2, 0, 2, down2)], [(False, 2, x2), (True, 1, y1), (True, 3, y3)]
    )
    up3, down3, x1, x3, y2, full = tie((up3, down3, x1, x3, y2, full))
    *full, top, bottom = gather(where, full, [(-3, 0, 2, up3), (3, 0, 2, down3)], [], True)
    up4, down4 = to_z(top, 1), to_z(bottom, -1)
    full = gather(where, full, [], [(False, 1, x1), (False, 3, x3), (True, 2, y2)])
    full = gather(where, full, [(-4, 0, 1, up4), (4, 1, 1, down4)], [])

    give = li_terms(1, *full)
    got = from_core(give)
    have = li_terms(0, *full)
    q2, mixed, states = block_states(have, got, fade)
    inside = inner(mixed, blocks)

    other = from_core(states)
    early = jnp.where(c == 0, states, other)
    late = jnp.where(c == 0, other, states)
    s0, s1, s2, s3 = early[0], late[0], early[1], late[1]
    total = s3 + one * (s2 + one * (s1 + one * s0))
    along_y = [total] + [from_y(total, k) for k in (3, 2, 1)]
    row_total = sum(within[d] * along_y[d] for d in range(4))
    before_y = sum(before[d - 1] * along_y[d] for d in (1, 2, 3))
    before_x = from_x_before(row_total, 1) + row_step * (
        from_x_before(row_total, 2) + row_step * from_x_before(row_total, 3)
    )
    at = before_y + to_row * before_x
    at1 = s0 + one * at
    at2 = s1 + one * at1
    at3 = s2 + one * at2
    start = jnp.stack([jnp.where(c == 0, at, at1), jnp.where(c == 0, at2, at3)])

    terms = logit_terms(start, inside, q2, log_row, coef_row, proj)
    terms = lax.all_to_all(terms, ("run", "chan"), 0, 0, tiled=True)
    return jnp.sum(terms.astype(F32), axis=0).astype(BF16)


def solution(mesh):
    chips = Mesh(mesh.devices.reshape(NL, NX, NY, NH, NC), ("chan",) + SEQ)
    in_specs = (
        P(SEQ),
        P(None, None, "chan"),
        P(None, None, "chan"),
        P(),
        P(SEQ, None, "chan"),
        P(),
        P(),
        P("chan", None),
    )
    out_specs = P(SEQ, "chan")
    return jax.shard_map(shards, mesh=chips, in_specs=in_specs, out_specs=out_specs, check_vma=False)
```

```python
import functools

import jax
import jax.numpy as jnp
from jax import lax
from jax.experimental import pallas as pl
from jax.experimental.pallas import tpu as pltpu
from jax.sharding import Mesh
from jax.sharding import PartitionSpec as P

F32 = jnp.float32
BF16 = jnp.bfloat16
GSIZE = 16
NX, NY, NH, NC, NL = 4, 4, 2, 2, 4
NZ = NH * NL
SEQ = ("x", "y", "run", "core")
HALO = 144
HIGHEST = lax.Precision.HIGHEST


def seq_of(x, y, h, c):
    return ((x * NY + y) * NH + h) * NC + c


COORDS = [
    (x, y, h, c) for x in range(NX) for y in range(NY) for h in range(NH) for c in range(NC)
]


def seq_pairs(move):
    return [(seq_of(*a), seq_of(*move(*a))) for a in COORDS]


def from_x(v, j):
    return lax.ppermute(v, SEQ, seq_pairs(lambda x, y, h, c: ((x - j) % NX, y, h, c)))


def from_y(v, j):
    return lax.ppermute(v, SEQ, seq_pairs(lambda x, y, h, c: (x, (y - j) % NY, h, c)))


def from_run(v):
    return lax.ppermute(v, SEQ, seq_pairs(lambda x, y, h, c: (x, y, 1 - h, c)))


def from_core(v):
    return lax.ppermute(v, SEQ, seq_pairs(lambda x, y, h, c: (x, y, h, 1 - c)))


def y_swap(step):
    return seq_pairs(lambda x, y, h, c: (x, y ^ step, h, c))


def x_swap(step):
    return seq_pairs(lambda x, y, h, c: (x ^ step, y, h, c))


def to_z(v, d):
    pairs = []
    for z in range(NZ):
        for x in range(NX):
            for y in range(NY):
                for c in range(NC):
                    t = (z + d) % NZ
                    pairs.append(
                        (
                            (z % NL) * len(COORDS) + seq_of(x, y, z // NL, c),
                            (t % NL) * len(COORDS) + seq_of(x, y, t // NL, c),
                        )
                    )
    return lax.ppermute(v, ("chan",) + SEQ, pairs)


def act_kernel(
    where, ids_ref, emb_ref, sf_ref, mr_ref, keep_ref, send_ref, hot, feats, bands, held
):
    rows = keep_ref.shape[0]
    ext = hot.shape[0]
    step = pl.program_id(0)
    core = where[3]
    yy = lax.rem(where[1] + step, NY)
    wide = pl.ds(pl.multiple_of(yy * 256, 256), 256)

    @pl.when(step == 0)
    def _():
        col = lax.broadcasted_iota(jnp.int32, hot.shape, 1)
        hot[...] = jnp.where(ids_ref[...] == col, 1.0, 0.0).astype(BF16)

    for j in range(3):
        feats[j] = jnp.dot(hot[...], emb_ref[j, :, wide], preferred_element_type=F32)

    reach = 128
    group = (lax.broadcasted_iota(jnp.int32, (128, 256), 1) // GSIZE) % 8
    for b in range(2):
        cols = slice(b * 128, (b + 1) * 128)
        lanes = pl.ds(pl.multiple_of(yy * 256 + b * 128, 128), 128)

        def short(j, start, n, cols=cols, lanes=lanes):
            total = sf_ref[j, 0:1, lanes] * feats[j, start : start + n, cols]
            for k in range(1, 7):
                tap = sf_ref[j, k : k + 1, lanes]
                total = total + tap * feats[j, start - k : start - k + n, cols]
            return total

        first = ext - rows - reach
        gated = (short(0, first, rows + reach) * short(1, first, rows + reach)).astype(BF16)
        window = jnp.concatenate([gated[:256], gated[128:384]], axis=1)
        filt = mr_ref[pl.ds(pl.multiple_of(yy * 16 + b * 8, 8), 8), :]
        for g in range(8):
            base = jnp.broadcast_to(filt[g : g + 1, :], (128, 256))
            bands[g * 128 : (g + 1) * 128, :] = pltpu.roll(
                base, 0, 1, stride=1, stride_axis=0
            ).astype(BF16)
        both = jnp.dot(bands[...], window, preferred_element_type=F32)
        medium = both[:128]
        for g in range(1, 8):
            medium = jnp.where(group == g, both[g * 128 : (g + 1) * 128], medium)
        v1 = short(2, ext - rows, rows)
        out = jnp.concatenate([v1[:128] * medium[:, :128], v1[128:] * medium[:, 128:]], axis=0)

        @pl.when(lax.rem(step, 2) == 0)
        def _(out=out, b=b):
            held[b] = out

        @pl.when(lax.rem(step, 2) == 1)
        def _(out=out, b=b):
            even = jnp.concatenate([held[b, :, :64], out[:, :64]], axis=1)
            odd = jnp.concatenate([held[b, :, 64:], out[:, 64:]], axis=1)
            to = pl.ds(pl.multiple_of(b * 256 + (step // 2) * 128, 128), 128)
            keep_ref[:, to] = jnp.where(core == 0, even, odd).astype(BF16)
            send_ref[:, to] = jnp.where(core == 0, odd, even).astype(BF16)


def activations(where, ids, emb, sf, mr_rows):
    ext = ids.shape[0]
    return pl.pallas_call(
        act_kernel,
        grid=(4,),
        out_shape=(jax.ShapeDtypeStruct((256, 512), BF16),) * 2,
        in_specs=[
            pl.BlockSpec(memory_space=pltpu.SMEM),
            pl.BlockSpec(memory_space=pltpu.VMEM),
            pl.BlockSpec(memory_space=pltpu.VMEM),
            pl.BlockSpec(memory_space=pltpu.VMEM),
            pl.BlockSpec(memory_space=pltpu.VMEM),
        ],
        out_specs=(pl.BlockSpec(memory_space=pltpu.VMEM),) * 2,
        scratch_shapes=[
            pltpu.VMEM((ext, 512), BF16),
            pltpu.VMEM((3, ext, 256), F32),
            pltpu.VMEM((1024, 256), BF16),
            pltpu.VMEM((2, 256, 128), F32),
        ],
        compiler_params=pltpu.CompilerParams(vmem_limit_bytes=12 * 2**20),
        cost_estimate=pl.CostEstimate(flops=4 * 10**9, bytes_accessed=8 * 10**6, transcendentals=0),
    )(where, ids, emb, sf, mr_rows)


def block_place(where, d):
    zz = lax.rem(where[4] + d + NZ, NZ)
    rows = pl.multiple_of((zz // NL) * 256, 256)
    lanes = pl.multiple_of(lax.rem(zz, NL) * 512, 512)
    return pl.ds(rows, 256), pl.ds(lanes, 512)


def gather_kernel(steps, plan, halves, where, *refs):
    n_in = len(steps) + len(plan)
    sources = refs[:n_in]
    outs = 4 if halves else 2
    a_ref, w_ref = refs[-1 - outs], refs[-outs]
    sem = refs[-1]
    x, h = where[0], where[2]
    copies = []
    for src, (d, first, count) in zip(sources, steps):
        rows, lanes = block_place(where, d)
        for p in range(count):
            copies.append((src.at[pl.ds(p * 256, 256), :], a_ref.at[first + p, rows, lanes]))
    for src, (own_run, at) in zip(sources[len(steps) :], plan):
        run = h if own_run else 1 - h
        for other in range(4):
            j, k = (other, at) if own_run else (at, other)
            row = lax.rem(x + j, NX) * 512 + run * 256 + k * 64
            rows = pl.ds(pl.multiple_of(row, 64), 64)
            copies.append((src.at[other], w_ref.at[:, rows, :]))
    if halves:
        copies.append((sources[0].at[pl.ds(0, 256), :], refs[-3]))
        copies.append((sources[1].at[pl.ds(256, 256), :], refs[-2]))
    copies = [pltpu.make_async_copy(a, b, sem.at[n]) for n, (a, b) in enumerate(copies)]
    for copy in copies:
        copy.start()
    for copy in copies:
        copy.wait()


def gather(where, full, blocks, pieces, halves=False):
    steps = [b[:3] for b in blocks]
    plan = [(own_run, at) for own_run, at, _ in pieces]
    operands = [b[3] for b in blocks] + [v for _, _, v in pieces]
    vmem = pl.BlockSpec(memory_space=pltpu.VMEM)
    alias = {}
    if full is not None:
        alias = {1 + len(operands): 0, 2 + len(operands): 1}
        operands += list(full)
    n_copies = sum(c for _, _, c in steps) + 4 * len(plan) + 2 * halves
    shapes = (
        jax.ShapeDtypeStruct((2, 512, 2048), BF16),
        jax.ShapeDtypeStruct((3, 2048, 512), BF16),
    )
    shapes += (jax.ShapeDtypeStruct((256, 512), BF16),) * (2 * halves)
    return pl.pallas_call(
        functools.partial(gather_kernel, steps, plan, halves),
        out_shape=shapes,
        in_specs=[pl.BlockSpec(memory_space=pltpu.SMEM)] + [vmem] * len(operands),
        out_specs=(vmem,) * len(shapes),
        scratch_shapes=[pltpu.SemaphoreType.DMA((n_copies,))],
        input_output_aliases=alias,
        compiler_params=pltpu.CompilerParams(vmem_limit_bytes=4 * 2**20),
        cost_estimate=pl.CostEstimate(flops=10**6, bytes_accessed=6 * 10**6, transcendentals=0),
    )(where, *operands)


def li_kernel(which, a_ref, w_ref, out_ref):
    for t in range(3):

        def step(m, _, t=t):
            rows = pl.ds(pl.multiple_of(m * 256, 256), 256)
            out_ref[t, rows, :] = jnp.dot(
                a_ref[which, rows, :], w_ref[t], preferred_element_type=F32
            ).astype(out_ref.dtype)
            return 0

        lax.fori_loop(0, 2, step, 0)


def li_terms(which, a_full, w_full):
    vmem = pl.BlockSpec(memory_space=pltpu.VMEM)
    return pl.pallas_call(
        functools.partial(li_kernel, which),
        out_shape=jax.ShapeDtypeStruct((3, 512, 512), BF16 if which else F32),
        in_specs=[vmem] * 2,
        out_specs=vmem,
        compiler_params=pltpu.CompilerParams(vmem_limit_bytes=8 * 2**20),
        cost_estimate=pl.CostEstimate(
            flops=33 * 10**8, bytes_accessed=10 * 10**6, transcendentals=0
        ),
    )(a_full, w_full)


def states_kernel(own_ref, got_ref, fade_ref, q_ref, mixed_ref, state_ref):
    q_ref[...] = own_ref[0] + got_ref[0].astype(F32)
    group = lax.broadcasted_iota(jnp.int32, (16, 128), 1) // GSIZE
    for b in range(4):
        cols = slice(b * 128, (b + 1) * 128)
        fade = fade_ref[cols, :]
        high = fade.astype(BF16)
        low = (fade - high.astype(F32)).astype(BF16)
        for m in range(2):
            rows = slice(m * 256, (m + 1) * 256)
            k2 = own_ref[1, rows, cols] + got_ref[1, rows, cols].astype(F32)
            v2 = own_ref[2, rows, cols] + got_ref[2, rows, cols].astype(F32)
            block = (k2 * v2).astype(BF16)
            mixed_ref[rows, cols] = block
            full = jnp.dot(high, block, preferred_element_type=F32) + jnp.dot(
                low, block, preferred_element_type=F32
            )
            state = full[:16]
            for g in range(1, 8):
                state = jnp.where(group == g, full[g * 16 : (g + 1) * 16], state)
            state_ref[m, :, cols] = state


def block_states(own, got, fade):
    vmem = pl.BlockSpec(memory_space=pltpu.VMEM)
    return pl.pallas_call(
        states_kernel,
        out_shape=(
            jax.ShapeDtypeStruct((512, 512), F32),
            jax.ShapeDtypeStruct((512, 512), BF16),
            jax.ShapeDtypeStruct((2, 16, 512), F32),
        ),
        in_specs=[vmem] * 3,
        out_specs=(vmem,) * 3,
        compiler_params=pltpu.CompilerParams(vmem_limit_bytes=12 * 2**20),
        cost_estimate=pl.CostEstimate(flops=5 * 10**8, bytes_accessed=5 * 10**6, transcendentals=0),
    )(own, got, fade)


def inner_kernel(x_ref, h_ref, out_ref):
    both = jnp.concatenate([x_ref[:256, :], x_ref[256:, :]], axis=1)
    group = (lax.broadcasted_iota(jnp.int32, (256, 256), 1) // GSIZE) % 8
    total = None
    for g in range(8):
        base = jnp.broadcast_to(h_ref[g : g + 1, :], (256, 512))
        block = pltpu.roll(base, 0, 1, stride=1, stride_axis=0)[:, :256].astype(BF16)
        part = jnp.dot(block, both, preferred_element_type=F32)
        total = part if g == 0 else jnp.where(group == g, part, total)
    out_ref[:256, :] = total[:, :128]
    out_ref[256:, :] = total[:, 128:]


def inner(mixed, base_rows):
    return pl.pallas_call(
        inner_kernel,
        grid=(4,),
        out_shape=jax.ShapeDtypeStruct((512, 512), F32),
        in_specs=[
            pl.BlockSpec((512, 128), lambda i: (0, i)),
            pl.BlockSpec((8, 512), lambda i: (i, 0)),
        ],
        out_specs=pl.BlockSpec((512, 128), lambda i: (0, i)),
        compiler_params=pltpu.CompilerParams(vmem_limit_bytes=12 * 2**20),
        cost_estimate=pl.CostEstimate(
            flops=43 * 10**8, bytes_accessed=2 * 10**6, transcendentals=0
        ),
    )(mixed, base_rows)


def logits_kernel(start_ref, inner_ref, q_ref, log_ref, coef_ref, proj_ref, out_ref, li_out):
    step = (lax.broadcasted_iota(jnp.int32, (256, 128), 0) + 1).astype(F32)
    row_group = lax.broadcasted_iota(jnp.int32, (128, 128), 0) // 16
    col_group = lax.broadcasted_iota(jnp.int32, (128, 128), 1) // GSIZE
    for b in range(4):
        cols = slice(b * 128, (b + 1) * 128)
        lead = coef_ref[:, cols] * jnp.exp(step * log_ref[:, cols])
        for m in range(2):
            tiled = jnp.concatenate([start_ref[m, :, cols]] * 8, axis=0)
            diag = jnp.where(row_group == col_group, tiled, 0.0)
            cross = jnp.dot(lead, diag, precision=HIGHEST, preferred_element_type=F32)
            rows = slice(m * 256, (m + 1) * 256)
            li_out[rows, cols] = (
                q_ref[rows, cols] * (inner_ref[rows, cols] + cross)
            ).astype(BF16)
    for m in range(2):
        part = jnp.dot(
            li_out[m * 256 : (m + 1) * 256, :], proj_ref[...], preferred_element_type=F32
        )
        for v in range(NL):
            out_ref[m * NL + v] = part[:, v * 128 : (v + 1) * 128].astype(BF16)


def logit_terms(start, inside, q2, log_row, coef_row, proj):
    vmem = pl.BlockSpec(memory_space=pltpu.VMEM)
    return pl.pallas_call(
        logits_kernel,
        out_shape=jax.ShapeDtypeStruct((NZ, 256, 128), BF16),
        in_specs=[vmem] * 6,
        out_specs=vmem,
        scratch_shapes=[pltpu.VMEM((512, 512), BF16)],
        compiler_params=pltpu.CompilerParams(vmem_limit_bytes=12 * 2**20),
        cost_estimate=pl.CostEstimate(
            flops=10**9, bytes_accessed=4 * 10**6, transcendentals=10**5
        ),
    )(start, inside, q2, log_row, coef_row, proj)


def shards(ids, embed_proj, short_filter, mr_filter, li_proj, residue, rate, out_proj):
    seq = lax.axis_index(SEQ)
    chan = lax.axis_index("chan")
    x, y, h, c = seq // 16, (seq // 4) % 4, (seq // 2) % 2, seq % 2
    z = h * NL + chan
    where = jnp.stack([x, y, h, c, z]).astype(jnp.int32)
    total_len = ids.shape[0] * lax.axis_size(SEQ)
    tie = lax.optimization_barrier

    halo = lax.ppermute(
        ids[ids.shape[0] - HALO :] + 1, SEQ, [(i, i + 1) for i in range(len(COORDS) - 1)]
    )
    weights = jnp.transpose(li_proj, (1, 0, 2))
    mine = lax.dynamic_slice_in_dim(weights, h * 512, 512, 2)
    theirs = lax.dynamic_slice_in_dim(weights, (1 - h) * 512, 512, 2)
    rows_b = from_run(theirs)
    ext_ids = jnp.concatenate([halo - 1, ids])[:, None]
    emb = jnp.transpose(embed_proj, (1, 0, 2))
    taps = jnp.transpose(short_filter, (1, 0, 2))
    filt = lax.dynamic_slice_in_dim(mr_filter, chan * 64, 64, 0).astype(F32)
    mr_rows = jnp.pad(filt[:, ::-1], ((0, 0), (1, 127)))
    a_x = [mine] + [from_x(mine, j) for j in (1, 2, 3)]
    ext_ids, rows_b, a_x = tie((ext_ids, rows_b, a_x))
    a_x = jnp.stack(a_x)
    b_y = jnp.stack([rows_b] + [from_y(rows_b, k) for k in (1, 2, 3)])
    keep, send = activations(where, ext_ids, emb, taps, mr_rows)
    rate, residue, out_proj, keep = tie((rate, residue, out_proj, keep))
    first = chan * 64 + h * 32
    log_all = -lax.dynamic_slice_in_dim(rate, first, 32, 0) / total_len
    coef = lax.dynamic_slice_in_dim(residue, first, 32, 0) * jnp.sqrt(-jnp.expm1(2.0 * log_all))
    lag = (512 - jnp.arange(512)) % 512
    power = jnp.exp(lag.astype(F32)[None, None, :] * log_all[:, :, None])
    base_rows = jnp.where(lag[None, :] < 256, jnp.sum(coef[:, :, None] * power, axis=1), 0.0)
    log_row = log_all.reshape(1, 512)
    coef_row = coef.reshape(1, 512)
    fade = jnp.exp(log_all.reshape(512, 1) * (255 - jnp.arange(256)).astype(F32)[None, :])
    log_ch = tie(jnp.repeat(log_all.T, GSIZE, axis=1))

    def decay(steps, keep=True):
        return jnp.where(keep, jnp.exp(steps * log_ch), 0.0)

    rows_of = 4.0 * ids.shape[0]
    one = decay(256.0)
    spans, offsets = [], []
    for size, upper, offset in (
        (1, y % 2, 0 * y),
        (2, y // 2, y % 2),
        (4, x % 2, y),
        (8, x // 2, y + 4 * (x % 2)),
    ):
        spans.append(decay(rows_of * size))
        offsets.append(decay(rows_of * offset.astype(F32), upper == 1))
    proj = lax.dynamic_slice_in_dim(out_proj, h * 512, 512, 0)
    own = jnp.concatenate([keep, from_core(send)], axis=0)

    full = gather(where, None, [(0, 0, 2, own)], [(True, 0, a_x), (False, 0, b_y)])
    up1, down1 = to_z(own, 1), to_z(own, -1)
    x2, y1, y3 = from_x(b_y, 2), from_y(a_x, 1), from_y(a_x, 3)
    params = (fade, one, spans, offsets, log_row, coef_row, proj, base_rows)
    up1, down1, params = tie((up1, down1, params))
    fade, one, spans, offsets, log_row, coef_row, proj, base_rows = params
    full = gather(where, full, [(-1, 0, 2, up1), (1, 0, 2, down1)], [])
    up2, down2 = to_z(up1, 1), to_z(down1, -1)
    x2, y1, y3, a_x, b_y = tie((x2, y1, y3, a_x, b_y))
    x1, x3, y2 = from_x(b_y, 1), from_x(b_y, 3), from_y(a_x, 2)
    full = gather(
        where, full, [(-2, 0, 2, up2), (2, 0, 2, down2)], [(False, 2, x2), (True, 1, y1), (True, 3, y3)]
    )
    up2, down2, x2 = tie((up2, down2, x2))
    up3, down3 = to_z(up2, 1), to_z(down2, -1)
    *full, top, bottom = gather(where, full, [(-3, 0, 2, up3), (3, 0, 2, down3)], [], True)
    up4, down4 = to_z(top, 1), to_z(bottom, -1)
    full = gather(where, full, [], [(False, 1, x1), (False, 3, x3), (True, 2, y2)])
    full = gather(where, full, [(-4, 0, 1, up4), (4, 1, 1, down4)], [])

    give = li_terms(1, *full)
    got = from_core(give)
    have = li_terms(0, *full)
    q2, mixed, states = block_states(have, got, fade)
    inside = inner(mixed, base_rows)

    other = from_core(states)
    early = jnp.where(c == 0, states, other)
    late = jnp.where(c == 0, other, states)
    s0, s1, s2, s3 = early[0], late[0], early[1], late[1]
    total = s3 + one * (s2 + one * (s1 + one * s0))
    at = jnp.zeros_like(total)
    for n, (bit, swap) in enumerate(
        ((y % 2, y_swap(1)), (y // 2, y_swap(2)), (x % 2, x_swap(1)), (x // 2, x_swap(2)))
    ):
        there = lax.ppermute(total, SEQ, swap)
        at = at + offsets[n] * there
        total = jnp.where(
            bit == 1, spans[n] * there + total, spans[n] * total + there
        )
    at1 = s0 + one * at
    at2 = s1 + one * at1
    at3 = s2 + one * at2
    start = jnp.stack([jnp.where(c == 0, at, at1), jnp.where(c == 0, at2, at3)])

    terms = logit_terms(start, inside, q2, log_row, coef_row, proj)
    terms = lax.all_to_all(terms, ("run", "chan"), 0, 0, tiled=True)
    return jnp.sum(terms.astype(F32), axis=0).astype(BF16)


def solution(mesh):
    chips = Mesh(mesh.devices.reshape(NL, NX, NY, NH, NC), ("chan",) + SEQ)
    in_specs = (
        P(SEQ),
        P(None, None, "chan"),
        P(None, None, "chan"),
        P(),
        P(SEQ, None, "chan"),
        P(),
        P(),
        P("chan", None),
    )
    out_specs = P(SEQ, "chan")
    return jax.shard_map(shards, mesh=chips, in_specs=in_specs, out_specs=out_specs, check_vma=False)
```

```python
import functools

import jax
import jax.numpy as jnp
from jax import lax
from jax.experimental import pallas as pl
from jax.experimental.pallas import tpu as pltpu
from jax.sharding import Mesh
from jax.sharding import PartitionSpec as P

F32 = jnp.float32
BF16 = jnp.bfloat16
GSIZE = 16
NX, NY, NH, NC, NL = 4, 4, 2, 2, 4
NZ = NH * NL
SEQ = ("x", "y", "run", "core")
HALO = 144
HIGHEST = lax.Precision.HIGHEST


def seq_of(x, y, h, c):
    return ((x * NY + y) * NH + h) * NC + c


COORDS = [
    (x, y, h, c) for x in range(NX) for y in range(NY) for h in range(NH) for c in range(NC)
]


def seq_pairs(move):
    return [(seq_of(*a), seq_of(*move(*a))) for a in COORDS]


def from_x(v, j):
    return lax.ppermute(v, SEQ, seq_pairs(lambda x, y, h, c: ((x - j) % NX, y, h, c)))


def from_y(v, j):
    return lax.ppermute(v, SEQ, seq_pairs(lambda x, y, h, c: (x, (y - j) % NY, h, c)))


def from_run(v):
    return lax.ppermute(v, SEQ, seq_pairs(lambda x, y, h, c: (x, y, 1 - h, c)))


def from_core(v):
    return lax.ppermute(v, SEQ, seq_pairs(lambda x, y, h, c: (x, y, h, 1 - c)))


def y_swap(step):
    return seq_pairs(lambda x, y, h, c: (x, y ^ step, h, c))


def x_swap(step):
    return seq_pairs(lambda x, y, h, c: (x ^ step, y, h, c))


def to_z(v, d):
    pairs = []
    for z in range(NZ):
        for x in range(NX):
            for y in range(NY):
                for c in range(NC):
                    t = (z + d) % NZ
                    pairs.append(
                        (
                            (z % NL) * len(COORDS) + seq_of(x, y, z // NL, c),
                            (t % NL) * len(COORDS) + seq_of(x, y, t // NL, c),
                        )
                    )
    return lax.ppermute(v, ("chan",) + SEQ, pairs)


def act_kernel(
    where, ids_ref, emb_ref, sf_ref, mr_ref, keep_ref, send_ref, hot, feats, bands, held
):
    rows = keep_ref.shape[0]
    ext = hot.shape[0]
    step = pl.program_id(0)
    core = where[3]
    yy = lax.rem(where[1] + step, NY)
    wide = pl.ds(pl.multiple_of(yy * 256, 256), 256)

    @pl.when(step == 0)
    def _():
        col = lax.broadcasted_iota(jnp.int32, hot.shape, 1)
        hot[...] = jnp.where(ids_ref[...] == col, 1.0, 0.0).astype(BF16)

    for j in range(3):
        feats[j] = jnp.dot(hot[...], emb_ref[j, :, wide], preferred_element_type=F32)

    reach = 128
    group = (lax.broadcasted_iota(jnp.int32, (128, 256), 1) // GSIZE) % 8
    for b in range(2):
        cols = slice(b * 128, (b + 1) * 128)
        lanes = pl.ds(pl.multiple_of(yy * 256 + b * 128, 128), 128)

        def short(j, start, n, cols=cols, lanes=lanes):
            total = sf_ref[j, 0:1, lanes] * feats[j, start : start + n, cols]
            for k in range(1, 7):
                tap = sf_ref[j, k : k + 1, lanes]
                total = total + tap * feats[j, start - k : start - k + n, cols]
            return total

        first = ext - rows - reach
        gated = (short(0, first, rows + reach) * short(1, first, rows + reach)).astype(BF16)
        window = jnp.concatenate([gated[:256], gated[128:384]], axis=1)
        filt = mr_ref[pl.ds(pl.multiple_of(yy * 16 + b * 8, 8), 8), :]
        for g in range(8):
            base = jnp.broadcast_to(filt[g : g + 1, :], (128, 256))
            bands[g * 128 : (g + 1) * 128, :] = pltpu.roll(
                base, 0, 1, stride=1, stride_axis=0
            ).astype(BF16)
        both = jnp.dot(bands[...], window, preferred_element_type=F32)
        medium = both[:128]
        for g in range(1, 8):
            medium = jnp.where(group == g, both[g * 128 : (g + 1) * 128], medium)
        v1 = short(2, ext - rows, rows)
        out = jnp.concatenate([v1[:128] * medium[:, :128], v1[128:] * medium[:, 128:]], axis=0)

        @pl.when(lax.rem(step, 2) == 0)
        def _(out=out, b=b):
            held[b] = out

        @pl.when(lax.rem(step, 2) == 1)
        def _(out=out, b=b):
            even = jnp.concatenate([held[b, :, :64], out[:, :64]], axis=1)
            odd = jnp.concatenate([held[b, :, 64:], out[:, 64:]], axis=1)
            to = pl.ds(pl.multiple_of(b * 256 + (step // 2) * 128, 128), 128)
            keep_ref[:, to] = jnp.where(core == 0, even, odd).astype(BF16)
            send_ref[:, to] = jnp.where(core == 0, odd, even).astype(BF16)


def activations(where, ids, emb, sf, mr_rows):
    ext = ids.shape[0]
    return pl.pallas_call(
        act_kernel,
        grid=(4,),
        out_shape=(jax.ShapeDtypeStruct((256, 512), BF16),) * 2,
        in_specs=[
            pl.BlockSpec(memory_space=pltpu.SMEM),
            pl.BlockSpec(memory_space=pltpu.VMEM),
            pl.BlockSpec(memory_space=pltpu.VMEM),
            pl.BlockSpec(memory_space=pltpu.VMEM),
            pl.BlockSpec(memory_space=pltpu.VMEM),
        ],
        out_specs=(pl.BlockSpec(memory_space=pltpu.VMEM),) * 2,
        scratch_shapes=[
            pltpu.VMEM((ext, 512), BF16),
            pltpu.VMEM((3, ext, 256), F32),
            pltpu.VMEM((1024, 256), BF16),
            pltpu.VMEM((2, 256, 128), F32),
        ],
        compiler_params=pltpu.CompilerParams(vmem_limit_bytes=12 * 2**20),
        cost_estimate=pl.CostEstimate(flops=4 * 10**9, bytes_accessed=8 * 10**6, transcendentals=0),
    )(where, ids, emb, sf, mr_rows)


def block_place(where, d):
    zz = lax.rem(where[4] + d + NZ, NZ)
    rows = pl.multiple_of((zz // NL) * 256, 256)
    lanes = pl.multiple_of(lax.rem(zz, NL) * 512, 512)
    return pl.ds(rows, 256), pl.ds(lanes, 512)


def gather_kernel(steps, plan, halves, where, *refs):
    n_in = len(steps) + len(plan)
    sources = refs[:n_in]
    outs = 4 if halves else 2
    a_ref, w_ref = refs[-1 - outs], refs[-outs]
    sem = refs[-1]
    x, h = where[0], where[2]
    copies = []
    for src, (d, first, count) in zip(sources, steps):
        rows, lanes = block_place(where, d)
        for p in range(count):
            copies.append((src.at[pl.ds(p * 256, 256), :], a_ref.at[first + p, rows, lanes]))
    for src, (own_run, at) in zip(sources[len(steps) :], plan):
        run = h if own_run else 1 - h
        for other in range(4):
            j, k = (other, at) if own_run else (at, other)
            row = lax.rem(x + j, NX) * 512 + run * 256 + k * 64
            rows = pl.ds(pl.multiple_of(row, 64), 64)
            copies.append((src.at[other], w_ref.at[:, rows, :]))
    if halves:
        copies.append((sources[0].at[pl.ds(0, 256), :], refs[-3]))
        copies.append((sources[1].at[pl.ds(256, 256), :], refs[-2]))
    copies = [pltpu.make_async_copy(a, b, sem.at[n]) for n, (a, b) in enumerate(copies)]
    for copy in copies:
        copy.start()
    for copy in copies:
        copy.wait()


def gather(where, full, blocks, pieces, halves=False):
    steps = [b[:3] for b in blocks]
    plan = [(own_run, at) for own_run, at, _ in pieces]
    operands = [b[3] for b in blocks] + [v for _, _, v in pieces]
    vmem = pl.BlockSpec(memory_space=pltpu.VMEM)
    alias = {}
    if full is not None:
        alias = {1 + len(operands): 0, 2 + len(operands): 1}
        operands += list(full)
    n_copies = sum(c for _, _, c in steps) + 4 * len(plan) + 2 * halves
    shapes = (
        jax.ShapeDtypeStruct((2, 512, 2048), BF16),
        jax.ShapeDtypeStruct((3, 2048, 512), BF16),
    )
    shapes += (jax.ShapeDtypeStruct((256, 512), BF16),) * (2 * halves)
    return pl.pallas_call(
        functools.partial(gather_kernel, steps, plan, halves),
        out_shape=shapes,
        in_specs=[pl.BlockSpec(memory_space=pltpu.SMEM)] + [vmem] * len(operands),
        out_specs=(vmem,) * len(shapes),
        scratch_shapes=[pltpu.SemaphoreType.DMA((n_copies,))],
        input_output_aliases=alias,
        compiler_params=pltpu.CompilerParams(vmem_limit_bytes=4 * 2**20),
        cost_estimate=pl.CostEstimate(flops=10**6, bytes_accessed=6 * 10**6, transcendentals=0),
    )(where, *operands)


def li_kernel(which, a_ref, w_ref, out_ref):
    for t in range(3):
        out_ref[t] = jnp.dot(
            a_ref[which], w_ref[t], preferred_element_type=F32
        ).astype(out_ref.dtype)


def li_terms(which, a_full, w_full):
    vmem = pl.BlockSpec(memory_space=pltpu.VMEM)
    return pl.pallas_call(
        functools.partial(li_kernel, which),
        out_shape=jax.ShapeDtypeStruct((3, 512, 512), BF16 if which else F32),
        in_specs=[vmem] * 2,
        out_specs=vmem,
        compiler_params=pltpu.CompilerParams(vmem_limit_bytes=12 * 2**20),
        cost_estimate=pl.CostEstimate(
            flops=33 * 10**8, bytes_accessed=10 * 10**6, transcendentals=0
        ),
    )(a_full, w_full)


def states_kernel(own_ref, got_ref, fade_ref, q_ref, mixed_ref, state_ref):
    q_ref[...] = own_ref[0] + got_ref[0].astype(F32)
    group = lax.broadcasted_iota(jnp.int32, (16, 128), 1) // GSIZE
    for b in range(4):
        cols = slice(b * 128, (b + 1) * 128)
        fade = fade_ref[cols, :]
        high = fade.astype(BF16)
        low = (fade - high.astype(F32)).astype(BF16)
        for m in range(2):
            rows = slice(m * 256, (m + 1) * 256)
            k2 = own_ref[1, rows, cols] + got_ref[1, rows, cols].astype(F32)
            v2 = own_ref[2, rows, cols] + got_ref[2, rows, cols].astype(F32)
            block = (k2 * v2).astype(BF16)
            mixed_ref[rows, cols] = block
            full = jnp.dot(high, block, preferred_element_type=F32) + jnp.dot(
                low, block, preferred_element_type=F32
            )
            state = full[:16]
            for g in range(1, 8):
                state = jnp.where(group == g, full[g * 16 : (g + 1) * 16], state)
            state_ref[m, :, cols] = state


def block_states(own, got, fade):
    vmem = pl.BlockSpec(memory_space=pltpu.VMEM)
    return pl.pallas_call(
        states_kernel,
        out_shape=(
            jax.ShapeDtypeStruct((512, 512), F32),
            jax.ShapeDtypeStruct((512, 512), BF16),
            jax.ShapeDtypeStruct((2, 16, 512), F32),
        ),
        in_specs=[vmem] * 3,
        out_specs=(vmem,) * 3,
        compiler_params=pltpu.CompilerParams(vmem_limit_bytes=12 * 2**20),
        cost_estimate=pl.CostEstimate(flops=5 * 10**8, bytes_accessed=5 * 10**6, transcendentals=0),
    )(own, got, fade)


def inner_kernel(x_ref, h_ref, out_ref):
    both = jnp.concatenate([x_ref[:256, :], x_ref[256:, :]], axis=1)
    group = (lax.broadcasted_iota(jnp.int32, (256, 256), 1) // GSIZE) % 8
    total = None
    for g in range(8):
        base = jnp.broadcast_to(h_ref[g : g + 1, :], (256, 512))
        block = pltpu.roll(base, 0, 1, stride=1, stride_axis=0)[:, :256].astype(BF16)
        part = jnp.dot(block, both, preferred_element_type=F32)
        total = part if g == 0 else jnp.where(group == g, part, total)
    out_ref[:256, :] = total[:, :128]
    out_ref[256:, :] = total[:, 128:]


def inner(mixed, base_rows):
    return pl.pallas_call(
        inner_kernel,
        grid=(4,),
        out_shape=jax.ShapeDtypeStruct((512, 512), F32),
        in_specs=[
            pl.BlockSpec((512, 128), lambda i: (0, i)),
            pl.BlockSpec((8, 512), lambda i: (i, 0)),
        ],
        out_specs=pl.BlockSpec((512, 128), lambda i: (0, i)),
        compiler_params=pltpu.CompilerParams(vmem_limit_bytes=12 * 2**20),
        cost_estimate=pl.CostEstimate(
            flops=43 * 10**8, bytes_accessed=2 * 10**6, transcendentals=0
        ),
    )(mixed, base_rows)


def logits_kernel(start_ref, inner_ref, q_ref, log_ref, coef_ref, proj_ref, out_ref, li_out):
    step = (lax.broadcasted_iota(jnp.int32, (256, 128), 0) + 1).astype(F32)
    row_group = lax.broadcasted_iota(jnp.int32, (128, 128), 0) // 16
    col_group = lax.broadcasted_iota(jnp.int32, (128, 128), 1) // GSIZE
    for b in range(4):
        cols = slice(b * 128, (b + 1) * 128)
        lead = coef_ref[:, cols] * jnp.exp(step * log_ref[:, cols])
        for m in range(2):
            tiled = jnp.concatenate([start_ref[m, :, cols]] * 8, axis=0)
            diag = jnp.where(row_group == col_group, tiled, 0.0)
            cross = jnp.dot(lead, diag, precision=HIGHEST, preferred_element_type=F32)
            rows = slice(m * 256, (m + 1) * 256)
            li_out[rows, cols] = (
                q_ref[rows, cols] * (inner_ref[rows, cols] + cross)
            ).astype(BF16)
    for m in range(2):
        part = jnp.dot(
            li_out[m * 256 : (m + 1) * 256, :], proj_ref[...], preferred_element_type=F32
        )
        for v in range(NL):
            out_ref[m * NL + v] = part[:, v * 128 : (v + 1) * 128].astype(BF16)


def logit_terms(start, inside, q2, log_row, coef_row, proj):
    vmem = pl.BlockSpec(memory_space=pltpu.VMEM)
    return pl.pallas_call(
        logits_kernel,
        out_shape=jax.ShapeDtypeStruct((NZ, 256, 128), BF16),
        in_specs=[vmem] * 6,
        out_specs=vmem,
        scratch_shapes=[pltpu.VMEM((512, 512), BF16)],
        compiler_params=pltpu.CompilerParams(vmem_limit_bytes=12 * 2**20),
        cost_estimate=pl.CostEstimate(
            flops=10**9, bytes_accessed=4 * 10**6, transcendentals=10**5
        ),
    )(start, inside, q2, log_row, coef_row, proj)


def shards(ids, embed_proj, short_filter, mr_filter, li_proj, residue, rate, out_proj):
    seq = lax.axis_index(SEQ)
    chan = lax.axis_index("chan")
    x, y, h, c = seq // 16, (seq // 4) % 4, (seq // 2) % 2, seq % 2
    z = h * NL + chan
    where = jnp.stack([x, y, h, c, z]).astype(jnp.int32)
    total_len = ids.shape[0] * lax.axis_size(SEQ)
    tie = lax.optimization_barrier

    marks = ids[ids.shape[0] - HALO :] + 1
    weights = jnp.transpose(li_proj, (1, 0, 2))
    mine = lax.dynamic_slice_in_dim(weights, h * 512, 512, 2)
    theirs = lax.dynamic_slice_in_dim(weights, (1 - h) * 512, 512, 2)
    mine, marks = tie((mine, marks))
    halo = lax.ppermute(marks, SEQ, [(i, i + 1) for i in range(len(COORDS) - 1)])
    rows_b = from_run(theirs)
    ext_ids = jnp.concatenate([halo - 1, ids])[:, None]
    emb = jnp.transpose(embed_proj, (1, 0, 2))
    taps = jnp.transpose(short_filter, (1, 0, 2))
    filt = lax.dynamic_slice_in_dim(mr_filter, chan * 64, 64, 0).astype(F32)
    mr_rows = jnp.pad(filt[:, ::-1], ((0, 0), (1, 127)))
    a_x = [mine] + [from_x(mine, j) for j in (1, 2, 3)]
    ext_ids, rows_b, a_x = tie((ext_ids, rows_b, a_x))
    a_x = jnp.stack(a_x)
    b_y = jnp.stack([rows_b] + [from_y(rows_b, k) for k in (1, 2, 3)])
    keep, send = activations(where, ext_ids, emb, taps, mr_rows)
    rate, residue, out_proj, keep = tie((rate, residue, out_proj, keep))
    first = chan * 64 + h * 32
    log_all = -lax.dynamic_slice_in_dim(rate, first, 32, 0) / total_len
    coef = lax.dynamic_slice_in_dim(residue, first, 32, 0) * jnp.sqrt(-jnp.expm1(2.0 * log_all))
    lag = (512 - jnp.arange(512)) % 512
    power = jnp.exp(lag.astype(F32)[None, None, :] * log_all[:, :, None])
    base_rows = jnp.where(lag[None, :] < 256, jnp.sum(coef[:, :, None] * power, axis=1), 0.0)
    log_row = log_all.reshape(1, 512)
    coef_row = coef.reshape(1, 512)
    fade = jnp.exp(log_all.reshape(512, 1) * (255 - jnp.arange(256)).astype(F32)[None, :])
    log_ch = tie(jnp.repeat(log_all.T, GSIZE, axis=1))

    def decay(steps, keep=True):
        return jnp.where(keep, jnp.exp(steps * log_ch), 0.0)

    rows_of = 4.0 * ids.shape[0]
    one = decay(256.0)
    spans, offsets = [], []
    for size, upper, offset in (
        (1, y % 2, 0 * y),
        (2, y // 2, y % 2),
        (4, x % 2, y),
        (8, x // 2, y + 4 * (x % 2)),
    ):
        spans.append(decay(rows_of * size))
        offsets.append(decay(rows_of * offset.astype(F32), upper == 1))
    proj = lax.dynamic_slice_in_dim(out_proj, h * 512, 512, 0)
    own = jnp.concatenate([keep, from_core(send)], axis=0)

    full = gather(where, None, [(0, 0, 2, own)], [(True, 0, a_x), (False, 0, b_y)])
    up1, down1 = to_z(own, 1), to_z(own, -1)
    x2, y1, y3 = from_x(b_y, 2), from_y(a_x, 1), from_y(a_x, 3)
    params = (fade, one, spans, offsets, log_row, coef_row, proj, base_rows)
    up1, down1, params = tie((up1, down1, params))
    fade, one, spans, offsets, log_row, coef_row, proj, base_rows = params
    full = gather(where, full, [(-1, 0, 2, up1), (1, 0, 2, down1)], [])
    up2, down2 = to_z(up1, 1), to_z(down1, -1)
    x2, y1, y3, a_x, b_y = tie((x2, y1, y3, a_x, b_y))
    x1, x3, y2 = from_x(b_y, 1), from_x(b_y, 3), from_y(a_x, 2)
    full = gather(
        where, full, [(-2, 0, 2, up2), (2, 0, 2, down2)], [(False, 2, x2), (True, 1, y1), (True, 3, y3)]
    )
    up2, down2, x2 = tie((up2, down2, x2))
    up3, down3 = to_z(up2, 1), to_z(down2, -1)
    *full, top, bottom = gather(where, full, [(-3, 0, 2, up3), (3, 0, 2, down3)], [], True)
    up4, down4 = to_z(top, 1), to_z(bottom, -1)
    full = gather(where, full, [], [(False, 1, x1), (False, 3, x3), (True, 2, y2)])
    full = gather(where, full, [(-4, 0, 1, up4), (4, 1, 1, down4)], [])

    give = li_terms(1, *full)
    got = from_core(give)
    have = li_terms(0, *full)
    q2, mixed, states = block_states(have, got, fade)
    inside = inner(mixed, base_rows)

    other = from_core(states)
    early = jnp.where(c == 0, states, other)
    late = jnp.where(c == 0, other, states)
    s0, s1, s2, s3 = early[0], late[0], early[1], late[1]
    total = s3 + one * (s2 + one * (s1 + one * s0))
    at = jnp.zeros_like(total)
    for n, (bit, swap) in enumerate(
        ((y % 2, y_swap(1)), (y // 2, y_swap(2)), (x % 2, x_swap(1)), (x // 2, x_swap(2)))
    ):
        there = lax.ppermute(total, SEQ, swap)
        at = at + offsets[n] * there
        total = jnp.where(
            bit == 1, spans[n] * there + total, spans[n] * total + there
        )
    at1 = s0 + one * at
    at2 = s1 + one * at1
    at3 = s2 + one * at2
    start = jnp.stack([jnp.where(c == 0, at, at1), jnp.where(c == 0, at2, at3)])

    terms = logit_terms(start, inside, q2, log_row, coef_row, proj)
    terms = lax.all_to_all(terms, ("run", "chan"), 0, 0, tiled=True)
    return jnp.sum(terms.astype(F32), axis=0).astype(BF16)


def solution(mesh):
    chips = Mesh(mesh.devices.reshape(NL, NX, NY, NH, NC), ("chan",) + SEQ)
    in_specs = (
        P(SEQ),
        P(None, None, "chan"),
        P(None, None, "chan"),
        P(),
        P(SEQ, None, "chan"),
        P(),
        P(),
        P("chan", None),
    )
    out_specs = P(SEQ, "chan")
    return jax.shard_map(shards, mesh=chips, in_specs=in_specs, out_specs=out_specs, check_vma=False)
```
